256 devices in a mesh: hst: 32 (over z, y), head: 8 (over x, core).
Axes of the slice: x: 4, y: 4, z: 8, core: 2. Of those that a mesh axis runs over, the one named last changes fastest.
Arguments:
- ctx_query: bfloat16 [32768, 8192], P(('hst', 'head')), may hold values from -180 to 180
- ctx_key: bfloat16 [32768, 1024], P(('hst', 'head')), may hold values from -6 to 6
- ctx_value: bfloat16 [32768, 1024], P(('hst', 'head')), may hold values from -6 to 6
- requests: bfloat16 [32, 256, 8192], P('hst', None, 'head'), may hold values from -180 to 180
- lengths: int32 [32], P('hst'), may hold values from 1 to 1024, as said below
- owner: int32 [32], replicated, may hold values from 0 to 31, each once
Outputs:
- context_out: bfloat16 [32768, 8192], P(('hst', 'head'))
- query_out: bfloat16 [256, 8192], P(None, 'head')
The draws below stay inside these ranges and needn't reach their ends.
Inputs may be any that keep to these rules, and one draw needn't show every extreme that they name: `lengths`: every block holds 1024 live tokens except the last block.
All inputs are finite; a program needn't handle non-finite values.
Results may differ from the reference program's by a relative error of at most 0.0031.
Values may be sent and summed in bfloat16 or wider, within the bound.
No kernel may reach another device: no remote copies, remote signals or barrier semaphores. Data moves between devices by JAX's collectives and lax.ppermute only.
A program may use at most 128 MiB of HBM per device.

```python
import jax
import jax.numpy as jnp
from jax import lax

H = 64
KV = 8
DH = 128
QTOK = 256
BLK = 1024
ANC = 512
NCTX = 32768
N_HST = 32


def key_rows(key):
    return jnp.clip(jax.random.normal(key, (N_HST * BLK, KV * DH), jnp.float32), -6.0, 6.0)


def draw_ctx_key(key, part):
    base = key_rows(key)
    return jnp.clip(base, -6.0, 6.0).astype(jnp.bfloat16)


def draw_ctx_query(key, part):
    key = jax.random.fold_in(key, 7)
    count = N_HST * BLK
    shape = (count, H * DH)
    rough = 2.5 * jax.random.normal(key, shape, jnp.float32)
    return jnp.clip(rough, -180.0, 180.0).astype(jnp.bfloat16)


def draw_requests(key, part):
    key = jax.random.fold_in(key, 13)
    shape = (N_HST, QTOK, H * DH)
    rough = 2.5 * jax.random.normal(key, shape, jnp.float32)
    return jnp.clip(rough, -180.0, 180.0).astype(jnp.bfloat16)


def draw_lengths(key, part):
    key = jax.random.fold_in(key, 5)
    final = jax.random.randint(key, (1,), 1, BLK + 1).astype(jnp.int32)
    return jnp.concatenate([jnp.full((N_HST - 1,), BLK, jnp.int32), final])


def shard_levels(key, extent, split, low, largest):
    gain, own = 1.0, jax.random.fold_in(key, 6)
    for axis_at, blocks in split:
        heights = jnp.exp(jax.random.uniform(jax.random.fold_in(own, axis_at), (blocks,), jnp.float32, low / len(split), largest / len(split)))
        gain = gain * jnp.repeat(heights, extent[axis_at] // blocks).reshape([-1 if axis == axis_at else 1 for axis in range(len(extent))])
    return gain


def normal_values(rng, shape, scale, reach, split=(), held_as=jnp.bfloat16):
    drawn = jax.random.normal(rng, shape, jnp.float32) * scale
    if len(split) > 0:
        drawn = shard_levels(rng, shape, split, -0.22, 0.18) * drawn
    return jnp.clip(drawn, min=-reach, max=reach).astype(held_as)


def setup_inputs(seed: int = 0) -> dict:
    key_of = jax.random.split(jax.random.key(seed), 7)
    return {
        "ctx_query": draw_ctx_query(jax.random.fold_in(key_of[6], 71), 0),
        "ctx_key": draw_ctx_key(jax.random.fold_in(key_of[6], 71), 0),
        "ctx_value": normal_values(key_of[2], (NCTX, KV * DH), 1.0, 6.0, ((0, 256),)),
        "requests": draw_requests(jax.random.fold_in(key_of[6], 71), 0),
        "lengths": draw_lengths(jax.random.fold_in(key_of[6], 71), 0),
        "owner": jax.random.permutation(key_of[5], N_HST).astype(jnp.int32),
    }


def head_attend(query_head, key_head, value_head, keep):
    scores = jnp.dot(query_head, key_head.T, preferred_element_type=jnp.float32) * (DH ** -0.5)
    scores = jnp.where(keep, scores, -1e30)
    top = jnp.max(scores, axis=1)
    weights = jnp.where(keep, jnp.exp(scores - top[:, None]), 0.0)
    total = jnp.sum(weights, axis=1)
    summed = jnp.dot(weights.astype(jnp.bfloat16), value_head, preferred_element_type=jnp.float32)
    return top, total, summed


def every_head(queries, keys, values, keep):
    group = H // KV

    def one_head(index):
        kv_index = index // group
        query_head = lax.dynamic_slice_in_dim(queries, index * DH, DH, 1)
        key_head = lax.dynamic_slice_in_dim(keys, kv_index * DH, DH, 1)
        value_head = lax.dynamic_slice_in_dim(values, kv_index * DH, DH, 1)
        return head_attend(query_head, key_head, value_head, keep)

    return lax.map(one_head, jnp.arange(H, dtype=jnp.int32))


def reference(ctx_query, ctx_key, ctx_value, requests, lengths, owner):
    anchor_key = ctx_key[:ANC]
    anchor_value = ctx_value[:ANC]
    positions = jnp.arange(BLK, dtype=jnp.int32)

    def one_block(block):
        start = (block * BLK).astype(jnp.int32)
        queries = lax.dynamic_slice_in_dim(ctx_query, start, BLK, 0)
        keys = jnp.concatenate([anchor_key, lax.dynamic_slice_in_dim(ctx_key, start, BLK, 0)], axis=0)
        values = jnp.concatenate([anchor_value, lax.dynamic_slice_in_dim(ctx_value, start, BLK, 0)], axis=0)
        length = lengths[block]
        causal = (positions[None, :] <= positions[:, None]) & (positions[None, :] < length)
        front = jnp.broadcast_to(block > 0, (BLK, ANC))
        keep = jnp.concatenate([front, causal], axis=1)
        top, total, summed = every_head(queries, keys, values, keep)
        live = positions < length
        safe = jnp.where(live[None, :], total, 1.0)
        result = jnp.where(live[None, :, None], summed / safe[:, :, None], 0.0)
        return result.transpose(1, 0, 2).reshape(BLK, H * DH).astype(jnp.bfloat16)

    context_out = lax.map(one_block, jnp.arange(N_HST, dtype=jnp.int32)).reshape(N_HST * BLK, H * DH)

    asked = lax.dynamic_index_in_dim(requests, owner[0], 0, keepdims=False)

    def block_part(block):
        start = (block * BLK).astype(jnp.int32)
        keys = lax.dynamic_slice_in_dim(ctx_key, start, BLK, 0)
        values = lax.dynamic_slice_in_dim(ctx_value, start, BLK, 0)
        keep = jnp.broadcast_to((positions < lengths[block])[None, :], (QTOK, BLK))
        return every_head(asked, keys, values, keep)

    def combine(carry, block):
        top_a, total_a, summed_a = carry
        top_b, total_b, summed_b = block_part(block)
        best = jnp.maximum(top_a, top_b)
        weight_a = jnp.exp(top_a - best)
        weight_b = jnp.exp(top_b - best)
        return (best, total_a * weight_a + total_b * weight_b,
                summed_a * weight_a[:, :, None] + summed_b * weight_b[:, :, None]), None

    first = block_part(jnp.int32(0))
    (top, total, summed), _ = lax.scan(combine, first, jnp.arange(1, N_HST, dtype=jnp.int32))
    query_out = (summed / total[:, :, None]).transpose(1, 0, 2).reshape(QTOK, H * DH).astype(jnp.bfloat16)
    return context_out, query_out
```

```python
import functools

import jax
import jax.numpy as jnp
from jax import lax
from jax.experimental import pallas as pl
from jax.experimental.pallas import tpu as pltpu
from jax.sharding import PartitionSpec as P

DH = 128
CORES = 2
NEG = -1e30
EXP2_SCALE = DH ** (-0.5) * 1.4426950408889634


def shift_chip(x, step, chips):
    size = chips * CORES
    return lax.ppermute(x, "head", [(i, (i + step * CORES) % size) for i in range(size)])


def swap_core(x, size):
    return lax.ppermute(x, "head", [(i, i ^ 1) for i in range(size)])


def spread_over_group(shard, chips):
    own = [shard] + [shift_chip(shard, step, chips) for step in range(1, chips)]
    return own + [swap_core(part, chips * CORES) for part in own]


def spread_anchor(kv, hst, head, n_hst, n_head):
    rows = kv.shape[0] // 2
    sources = n_head // 2
    lower, upper = kv[:rows], kv[rows:]
    moved = lax.ppermute(upper, ("hst", "head"), [(h, h + sources) for h in range(sources)])
    part = jnp.where(head < sources, lower, moved)
    ny, nz = 4, n_hst // 4
    z, y = hst // ny, hst % ny

    def send(x, pairs, axis_of):
        return lax.ppermute(x, "hst", [(axis_of(a), axis_of(b)) for a, b in pairs])

    along_z = lambda a: a * ny
    first, second = send(part, [(0, 3)], along_z), send(part, [(0, 5)], along_z)
    part = jnp.where(z == 3, first, jnp.where(z == 5, second, part))
    first = send(part, [(0, 1), (3, 4), (5, 6)], along_z)
    second = send(part, [(0, 7), (3, 2)], along_z)
    part = jnp.where((z == 1) | (z == 4) | (z == 6), first, jnp.where((z == 7) | (z == 2), second, part))
    for_y = [lax.ppermute(part, "hst", [(k * ny, k * ny + to) for k in range(nz)]) for to in (1, 3, 2)]
    return jnp.where(
        y == 1, for_y[0], jnp.where(y == 3, for_y[1], jnp.where(y == 2, for_y[2], part))
    )


def query_kernel(scal, asked, *refs):
    shards = 8
    keys, values, out = refs[:shards], refs[shards : 2 * shards], refs[2 * shards]
    length = scal[1]
    key = jnp.concatenate([r[...] for r in keys], axis=0)
    value = jnp.concatenate([r[...] for r in values], axis=0)
    rows = asked.shape[0]
    heads = asked.shape[1] // DH
    width = keys[0].shape[0]
    lane = lax.broadcasted_iota(jnp.int32, (1, width), 1)
    place = jnp.concatenate([lane + scal[2 + j] * width for j in range(shards)], axis=1)
    keep = place < length
    column = lax.broadcasted_iota(jnp.int32, (rows, DH), 1)
    stats = jnp.zeros((rows, DH), jnp.float32)
    for a in range(heads):
        query = asked[:, a * DH : (a + 1) * DH]
        score = lax.dot_general(query, key, (((1,), (1,)), ((), ())), preferred_element_type=jnp.float32)
        score = jnp.where(keep, score, NEG)
        top = jnp.max(score, axis=1, keepdims=True)
        weight = jnp.exp2((score - top) * EXP2_SCALE)
        total = jnp.sum(weight, axis=1, keepdims=True)
        summed = jnp.dot(weight.astype(jnp.bfloat16), value, preferred_element_type=jnp.float32)
        out[:, a * DH : (a + 1) * DH] = summed
        stats = jnp.where(column == a, top * EXP2_SCALE, stats)
        stats = jnp.where(column == heads + a, total, stats)
    out[:, heads * DH :] = stats


def query_part(scal, asked, shards):
    rows, cols = asked.shape
    width = shards[0].shape[0]
    kv_heads = shards[0].shape[1] // (2 * DH)
    key_spec = pl.BlockSpec((width, DH), lambda i, s: (0, s[0]))
    value_spec = pl.BlockSpec((width, DH), lambda i, s: (0, kv_heads + s[0]))
    return pl.pallas_call(
        query_kernel,
        out_shape=jax.ShapeDtypeStruct((rows, cols + DH), jnp.float32),
        grid_spec=pltpu.PrefetchScalarGridSpec(
            num_scalar_prefetch=1,
            grid=(1,),
            in_specs=[pl.BlockSpec((rows, cols), lambda i, s: (0, 0))]
            + [key_spec] * len(shards)
            + [value_spec] * len(shards),
            out_specs=pl.BlockSpec((rows, cols + DH), lambda i, s: (0, 0)),
        ),
        compiler_params=pltpu.CompilerParams(vmem_limit_bytes=40 * 2**20),
        cost_estimate=pl.CostEstimate(flops=2**31, bytes_accessed=2**22, transcendentals=2**21),
        name="query_part",
    )(scal, asked, *shards, *shards)


def merge_kernel(parts, out):
    heads = out.shape[1] // DH
    n = parts.shape[0]
    for a in range(heads):
        top = parts[:, :, heads * DH + a : heads * DH + a + 1]
        total = parts[:, :, heads * DH + heads + a : heads * DH + heads + a + 1]
        best = jnp.max(top, axis=0, keepdims=True)
        scale = jnp.exp2(top - best)
        total_all = jnp.sum(total * scale, axis=0)
        summed = jnp.sum(parts[:, :, a * DH : (a + 1) * DH] * scale, axis=0)
        out[:, a * DH : (a + 1) * DH] = (summed / total_all).astype(out.dtype)


def merge_parts(parts):
    n, rows, cols = parts.shape
    return pl.pallas_call(
        merge_kernel,
        out_shape=jax.ShapeDtypeStruct((rows, cols - DH), jnp.bfloat16),
        compiler_params=pltpu.CompilerParams(vmem_limit_bytes=40 * 2**20),
        cost_estimate=pl.CostEstimate(flops=2**20, bytes_accessed=2**21, transcendentals=2**10),
        name="merge_parts",
    )(parts)


def context_kernel(scal, query, *refs):
    shards = 8
    keys, values = refs[:shards], refs[shards : 2 * shards]
    front_keys, front_values = refs[2 * shards : 3 * shards], refs[3 * shards : 4 * shards]
    out = refs[4 * shards]
    own, length, hst = scal[0], scal[1], scal[10]
    rows = query.shape[0]
    heads = query.shape[1] // DH
    stack = 4
    many = stack * rows
    key = jnp.concatenate([r[...] for r in keys] + [r[...] for r in front_keys], axis=0)
    value = jnp.concatenate([r[...] for r in values] + [r[...] for r in front_values], axis=0)
    front = front_keys[0].shape[0] * shards
    row = lax.broadcasted_iota(jnp.int32, (many, rows), 0) % rows
    lane = lax.broadcasted_iota(jnp.int32, (many, rows), 1)
    diagonal = lane <= row
    bias = [jnp.zeros((1, rows), jnp.float32)]
    for j in range(1, shards):
        bias.append(jnp.full((1, rows), jnp.where(scal[2 + j] < own, 0.0, NEG), jnp.float32))
    bias.append(jnp.full((1, front), jnp.where(hst > 0, 0.0, NEG), jnp.float32))
    bias = jnp.concatenate(bias, axis=1)
    place = own * rows + lax.broadcasted_iota(jnp.int32, (many, 1), 0) % rows
    live = place < length
    for part in range(heads // stack):
        columns = [slice((part * stack + a) * DH, (part * stack + a + 1) * DH) for a in range(stack)]
        q = jnp.concatenate([query[:, c] for c in columns], axis=0)
        score = lax.dot_general(q, key, (((1,), (1,)), ((), ())), preferred_element_type=jnp.float32)
        score = jnp.concatenate(
            [jnp.where(diagonal, score[:, :rows], NEG), score[:, rows:] + bias[:, rows:]], axis=1
        )
        top = jnp.max(score, axis=1, keepdims=True)
        weight = jnp.exp2((score - top) * EXP2_SCALE)
        total = jnp.sum(weight, axis=1, keepdims=True)
        summed = jnp.dot(weight.astype(jnp.bfloat16), value, preferred_element_type=jnp.float32)
        result = jnp.where(live, summed / total, 0.0).astype(out.dtype)
        for a, c in enumerate(columns):
            out[:, c] = result[a * rows : (a + 1) * rows]


def context_part(scal, query, shards, fronts):
    rows, cols = query.shape
    kv_heads = shards[0].shape[1] // (2 * DH)
    group = cols // kv_heads

    def specs(parts, offset):
        return [
            pl.BlockSpec((p.shape[0], DH), lambda g, s: (0, g + offset)) for p in parts
        ]

    return pl.pallas_call(
        context_kernel,
        out_shape=jax.ShapeDtypeStruct((rows, cols), jnp.bfloat16),
        grid_spec=pltpu.PrefetchScalarGridSpec(
            num_scalar_prefetch=1,
            grid=(kv_heads,),
            in_specs=[pl.BlockSpec((rows, group), lambda g, s: (0, g))]
            + specs(shards, 0)
            + specs(shards, kv_heads)
            + specs(fronts, 0)
            + specs(fronts, kv_heads),
            out_specs=pl.BlockSpec((rows, group), lambda g, s: (0, g)),
        ),
        compiler_params=pltpu.CompilerParams(vmem_limit_bytes=48 * 2**20),
        cost_estimate=pl.CostEstimate(flops=2**34, bytes_accessed=2**23, transcendentals=2**24),
        name="context_part",
    )(scal, query, *shards, *shards, *fronts, *fronts)


def per_device(n_hst, n_head, ctx_query, ctx_key, ctx_value, requests, lengths, owner):
    hst, head = lax.axis_index("hst"), lax.axis_index("head")
    chips = n_head // CORES
    pieces = requests[0].reshape(n_hst, -1, requests.shape[2])
    scattered = lax.all_to_all(pieces, "hst", 0, 0)
    piece = lax.dynamic_index_in_dim(scattered, owner[0], 0, False)
    asked = lax.all_to_all(jnp.broadcast_to(piece[None], pieces.shape), "hst", 0, 0)
    asked = asked.reshape(requests.shape[1:])
    kv = jnp.concatenate([ctx_key, ctx_value], axis=1)
    shards = spread_over_group(kv, chips)
    fronts = spread_over_group(spread_anchor(kv, hst, head, n_hst, n_head), chips)
    x, core = head // CORES, head % CORES
    places = [((x - step) % chips) * CORES + c for c in (core, 1 - core) for step in range(chips)]
    scal = jnp.stack([head, lengths[0]] + places + [hst]).astype(jnp.int32)
    part = query_part(scal, asked, shards)
    parts = lax.all_to_all(part.reshape(n_hst, -1, part.shape[1]), "hst", 0, 0)
    context_out = context_part(scal, ctx_query, shards, fronts)
    done = merge_parts(parts)
    query_out = lax.all_to_all(jnp.broadcast_to(done[None], (n_hst,) + done.shape), "hst", 0, 0)
    return context_out, query_out.reshape(requests.shape[1:])


def solution(mesh):
    placed = (
        P(("hst", "head"), None),
        P(("hst", "head"), None),
        P(("hst", "head"), None),
        P("hst", None, "head"),
        P("hst"),
        P(),
    )
    return jax.shard_map(
        functools.partial(per_device, mesh.shape["hst"], mesh.shape["head"]),
        mesh=mesh,
        in_specs=placed,
        out_specs=(P(("hst", "head"), None), P(None, "head")),
        check_vma=False,
    )
```

```python
import functools

import jax
import jax.numpy as jnp
from jax import lax
from jax.experimental import pallas as pl
from jax.experimental.pallas import tpu as pltpu
from jax.sharding import PartitionSpec as P

DH = 128
CORES = 2
NEG = -1e30
EXP2_SCALE = DH ** (-0.5) * 1.4426950408889634


def spread_over_group(shard, chips):
    size = chips * CORES
    ring = [
        lax.ppermute(shard, "head", [(i, (i + step * CORES) % size) for i in range(size)])
        for step in range(1, chips)
    ]
    near = jnp.concatenate([shard] + ring, axis=0)
    return near, lax.ppermute(near, "head", [(i, i ^ 1) for i in range(size)])


def spread_anchor(kv, hst, head, n_hst, n_head, ny):
    rows = kv.shape[0] // 2
    sources = n_head // 2
    moved = lax.ppermute(kv[rows:], ("hst", "head"), [(h, h + sources) for h in range(sources)])
    part = jnp.where(head < sources, kv[:rows], moved)
    z, y = hst // ny, hst % ny

    def send(x, pairs):
        return lax.ppermute(x, "hst", [(a * ny, b * ny) for a, b in pairs])

    first, second = send(part, [(0, 3)]), send(part, [(0, 5)])
    part = jnp.where(z == 3, first, jnp.where(z == 5, second, part))
    first, second = send(part, [(0, 1), (3, 4), (5, 6)]), send(part, [(0, 7), (3, 2)])
    part = jnp.where((z == 1) | (z == 4) | (z == 6), first, jnp.where((z == 7) | (z == 2), second, part))
    groups = range(n_hst // ny)
    first, second, third = (
        lax.ppermute(part, "hst", [(k * ny, k * ny + to) for k in groups]) for to in (1, 3, 2)
    )
    return jnp.where(y == 1, first, jnp.where(y == 3, second, jnp.where(y == 2, third, part)))


def pieces_of(x):
    parts = []
    for _ in range(3):
        parts.append(x.astype(jnp.bfloat16).astype(jnp.float32))
        x = x - parts[-1]
    return parts


def query_kernel(shards, scal, asked, near_key, far_key, near_value, far_value, after, out):
    length = scal[1]
    rows, heads = asked.shape[0], asked.shape[1] // DH
    key = jnp.concatenate([near_key[...], far_key[...]], axis=0)
    value = jnp.concatenate([near_value[...], far_value[...]], axis=0)
    width = key.shape[0] // shards
    lane = lax.broadcasted_iota(jnp.int32, (1, width), 1)
    keep = jnp.concatenate([lane + scal[3 + j] * width for j in range(shards)], axis=1) < length
    column = lax.broadcasted_iota(jnp.int32, (rows, DH), 1)
    stats = jnp.zeros((rows, DH), jnp.float32)
    for a in range(heads):
        query = asked[:, a * DH : (a + 1) * DH]
        score = lax.dot_general(query, key, (((1,), (1,)), ((), ())), preferred_element_type=jnp.float32)
        score = jnp.where(keep, score, NEG)
        top = jnp.max(score, axis=1, keepdims=True)
        weight = jnp.exp2((score - top) * EXP2_SCALE)
        total = jnp.sum(weight, axis=1, keepdims=True)
        summed = jnp.dot(weight.astype(jnp.bfloat16), value, preferred_element_type=jnp.float32)
        reach = jnp.max(jnp.abs(summed), axis=1, keepdims=True)
        power = jnp.ceil(jnp.log2(jnp.maximum(reach, 1e-36)))
        out[:, a * DH : (a + 1) * DH] = summed * jnp.exp2(-power)
        values = pieces_of(top * EXP2_SCALE) + pieces_of(total) + [power]
        for at, stat in enumerate(values):
            stats = jnp.where(column == at * heads + a, stat, stats)
    out[:, heads * DH :] = stats


def query_part(scal, asked, near, far, shards, after):
    rows, cols = asked.shape
    width = near.shape[0]
    kv_heads = near.shape[1] // (2 * DH)
    key = pl.BlockSpec((width, DH), lambda i, s: (0, s[0]))
    value = pl.BlockSpec((width, DH), lambda i, s: (0, kv_heads + s[0]))
    return pl.pallas_call(
        functools.partial(query_kernel, shards),
        out_shape=jax.ShapeDtypeStruct((rows, cols + DH), jnp.float32),
        grid_spec=pltpu.PrefetchScalarGridSpec(
            num_scalar_prefetch=1,
            grid=(1,),
            in_specs=[
                pl.BlockSpec((rows, cols), lambda i, s: (0, 0)),
                key,
                key,
                value,
                value,
                pl.BlockSpec(memory_space=pl.ANY),
            ],
            out_specs=pl.BlockSpec((rows, cols + DH), lambda i, s: (0, 0)),
        ),
        compiler_params=pltpu.CompilerParams(vmem_limit_bytes=40 * 2**20),
        cost_estimate=pl.CostEstimate(flops=2**31, bytes_accessed=2**22, transcendentals=2**21),
        name="query_part",
    )(scal, asked, near, far, near, far, after)


def merge_kernel(parts, out):
    heads = out.shape[1] // DH

    def stat(at, a):
        lane = heads * DH + at * heads + a
        return parts[:, :, lane : lane + 1]

    for a in range(heads):
        top = stat(0, a) + stat(1, a) + stat(2, a)
        total = stat(3, a) + stat(4, a) + stat(5, a)
        best = jnp.max(top, axis=0, keepdims=True)
        scale = jnp.exp2(top - best)
        total_all = jnp.sum(total * scale, axis=0)
        scale = scale * jnp.exp2(stat(6, a))
        summed = jnp.sum(parts[:, :, a * DH : (a + 1) * DH] * scale, axis=0)
        out[:, a * DH : (a + 1) * DH] = (summed / total_all).astype(out.dtype)


def merge_parts(parts):
    n, rows, cols = parts.shape
    return pl.pallas_call(
        merge_kernel,
        out_shape=jax.ShapeDtypeStruct((rows, cols - DH), jnp.bfloat16),
        compiler_params=pltpu.CompilerParams(vmem_limit_bytes=40 * 2**20),
        cost_estimate=pl.CostEstimate(flops=2**20, bytes_accessed=2**21, transcendentals=2**10),
        name="merge_parts",
    )(parts)


def context_kernel(shards, scal, query, *refs):
    keys, values, out, value = refs[:4], refs[4:8], refs[8], refs[9]
    own, length, hst = scal[0], scal[1], scal[2]
    rows, heads = query.shape[0], query.shape[1] // DH
    key = jnp.concatenate([r[...] for r in keys], axis=0)
    value[:, :DH] = jnp.concatenate([r[...] for r in values], axis=0)
    many = key.shape[0]

    @pl.when(pl.program_id(0) == 0)
    def _():
        value[:, DH:] = jnp.ones((many, DH), jnp.bfloat16)

    row = lax.broadcasted_iota(jnp.int32, (rows, rows), 0)
    diagonal = lax.broadcasted_iota(jnp.int32, (rows, rows), 1) <= row
    dropped = [jnp.where(scal[3 + j] < own, 0.0, NEG) for j in range(1, shards)]
    bias = [jnp.full((1, rows), d, jnp.float32) for d in dropped]
    front = many - shards * rows
    bias = jnp.concatenate(bias + [jnp.full((1, front), jnp.where(hst > 0, 0.0, NEG), jnp.float32)], axis=1)
    live = own * rows + row < length
    for a in range(heads):
        column = slice(a * DH, (a + 1) * DH)
        score = lax.dot_general(
            query[:, column], key, (((1,), (1,)), ((), ())), preferred_element_type=jnp.float32
        )
        score = jnp.concatenate(
            [jnp.where(diagonal, score[:, :rows], NEG), score[:, rows:] + bias], axis=1
        )
        top = jnp.max(score, axis=1, keepdims=True)
        weight = jnp.exp2((score - top) * EXP2_SCALE).astype(jnp.bfloat16)
        summed = jnp.dot(weight, value[...], preferred_element_type=jnp.float32)
        out[:, column] = jnp.where(live, summed[:, :DH] / summed[:, DH:], 0.0).astype(out.dtype)


def context_part(scal, query, parts, shards):
    rows, cols = query.shape
    kv_heads = parts[0].shape[1] // (2 * DH)
    group = cols // kv_heads

    def specs(offset):
        return [pl.BlockSpec((p.shape[0], DH), lambda g, s: (0, g + offset)) for p in parts]

    wide = pl.BlockSpec((rows, group), lambda g, s: (0, g))
    return pl.pallas_call(
        functools.partial(context_kernel, shards),
        out_shape=jax.ShapeDtypeStruct((rows, cols), jnp.bfloat16),
        grid_spec=pltpu.PrefetchScalarGridSpec(
            num_scalar_prefetch=1,
            grid=(kv_heads,),
            in_specs=[wide] + specs(0) + specs(kv_heads),
            out_specs=wide,
            scratch_shapes=[pltpu.VMEM((sum(p.shape[0] for p in parts), 2 * DH), jnp.bfloat16)],
        ),
        compiler_params=pltpu.CompilerParams(vmem_limit_bytes=48 * 2**20),
        cost_estimate=pl.CostEstimate(flops=2**34, bytes_accessed=2**23, transcendentals=2**24),
        name="context_part",
    )(scal, query, *parts, *parts)


def per_device(n_hst, n_head, ny, ctx_query, ctx_key, ctx_value, requests, lengths, owner):
    hst, head = lax.axis_index("hst"), lax.axis_index("head")
    chips = n_head // CORES
    pieces = requests[0].reshape(n_hst, -1, requests.shape[2])
    scattered = lax.all_to_all(pieces, "hst", 0, 0)
    piece = lax.dynamic_index_in_dim(scattered, owner[0], 0, False)
    asked = lax.all_to_all(jnp.broadcast_to(piece[None], pieces.shape), "hst", 0, 0)
    asked = asked.reshape(requests.shape[1:])
    kv = jnp.concatenate([ctx_key, ctx_value], axis=1)
    near, far = spread_over_group(kv, chips)
    anchor = spread_anchor(kv, hst, head, n_hst, n_head, ny)
    near_anchor, far_anchor = spread_over_group(anchor, chips)
    x, core = head // CORES, head % CORES
    places = [((x - step) % chips) * CORES + c for c in (core, 1 - core) for step in range(chips)]
    scal = jnp.stack([head, lengths[0], hst] + places).astype(jnp.int32)
    part = query_part(scal, asked, near, far, n_head, anchor).astype(jnp.float16)
    parts = lax.all_to_all(part.reshape(n_hst, -1, part.shape[1]), "hst", 0, 0)
    done = merge_parts(parts.astype(jnp.float32))
    query_out = lax.all_to_all(jnp.broadcast_to(done[None], (n_hst,) + done.shape), "hst", 0, 0)
    context_out = context_part(scal, ctx_query, [near, far, near_anchor, far_anchor], n_head)
    return context_out, query_out.reshape(requests.shape[1:])


def solution(mesh):
    placed = (
        P(("hst", "head"), None),
        P(("hst", "head"), None),
        P(("hst", "head"), None),
        P("hst", None, "head"),
        P("hst"),
        P(),
    )
    return jax.shard_map(
        functools.partial(per_device, mesh.shape["hst"], mesh.shape["head"], 4),
        mesh=mesh,
        in_specs=placed,
        out_specs=(P(("hst", "head"), None), P(None, "head")),
        check_vma=False,
    )
```

```python
import functools

import jax
import jax.numpy as jnp
from jax import lax
from jax.experimental import pallas as pl
from jax.experimental.pallas import tpu as pltpu
from jax.sharding import PartitionSpec as P

DH = 128
CORES = 2
NEG = -1e30
EXP2_SCALE = DH ** (-0.5) * 1.4426950408889634


def spread_over_group(shard, chips):
    size = chips * CORES
    ring = [
        lax.ppermute(shard, "head", [(i, (i + step * CORES) % size) for i in range(size)])
        for step in range(1, chips)
    ]
    near = jnp.concatenate([shard] + ring, axis=0)
    return near, lax.ppermute(near, "head", [(i, i ^ 1) for i in range(size)])


def spread_anchor(kv, hst, head, n_hst, n_head, ny):
    rows = kv.shape[0] // 2
    sources = n_head // 2
    moved = lax.ppermute(kv[rows:], ("hst", "head"), [(h, h + sources) for h in range(sources)])
    part = jnp.where(head < sources, kv[:rows], moved)
    z, y = hst // ny, hst % ny

    def send(x, pairs):
        return lax.ppermute(x, "hst", [(a * ny, b * ny) for a, b in pairs])

    first, second = send(part, [(0, 3)]), send(part, [(0, 5)])
    part = jnp.where(z == 3, first, jnp.where(z == 5, second, part))
    first, second = send(part, [(0, 1), (3, 4), (5, 6)]), send(part, [(0, 7), (3, 2)])
    part = jnp.where((z == 1) | (z == 4) | (z == 6), first, jnp.where((z == 7) | (z == 2), second, part))
    groups = range(n_hst // ny)
    first, second, third = (
        lax.ppermute(part, "hst", [(k * ny, k * ny + to) for k in groups]) for to in (1, 3, 2)
    )
    return jnp.where(y == 1, first, jnp.where(y == 3, second, jnp.where(y == 2, third, part)))


def pieces_of(x):
    parts = []
    for _ in range(3):
        parts.append(x.astype(jnp.bfloat16).astype(jnp.float32))
        x = x - parts[-1]
    return parts


def query_kernel(shards, scal, asked, near_key, far_key, near_value, far_value, after, out, value):
    length = scal[1]
    rows, cols = asked.shape
    heads = cols // DH
    key = jnp.concatenate([near_key[...], far_key[...]], axis=0)
    many = key.shape[0]
    value[:, :DH] = jnp.concatenate([near_value[...], far_value[...]], axis=0)
    value[:, DH:] = jnp.ones((many, DH), jnp.bfloat16)
    width = many // shards
    lane = lax.broadcasted_iota(jnp.int32, (1, width), 1)
    keep = jnp.concatenate([lane + scal[3 + j] * width for j in range(shards)], axis=1) < length
    some = 128
    column = lax.broadcasted_iota(jnp.int32, (some, DH), 1)
    high = out.shape[1]
    for first in range(0, rows, some):
        to = slice(first // high, (first + some) // high)
        stats = jnp.zeros((some, DH), jnp.float32)
        for a in range(heads):
            mine = slice(a * DH, (a + 1) * DH)
            score = lax.dot_general(
                asked[first : first + some, mine],
                key,
                (((1,), (1,)), ((), ())),
                preferred_element_type=jnp.float32,
            )
            score = jnp.where(keep, score, NEG)
            top = jnp.max(score, axis=1, keepdims=True)
            weight = jnp.exp2((score - top) * EXP2_SCALE).astype(jnp.bfloat16)
            both = jnp.dot(weight, value[...], preferred_element_type=jnp.float32)
            summed, total = both[:, :DH], both[:, DH:]
            reach = jnp.max(jnp.abs(summed), axis=1, keepdims=True)
            power = jnp.ceil(jnp.log2(jnp.maximum(reach, 1e-36)))
            out[to, :, mine] = (summed * jnp.exp2(-power)).reshape(some // high, high, DH)
            values = pieces_of(top * EXP2_SCALE) + pieces_of(total) + [power]
            for at, stat in enumerate(values):
                stats = jnp.where(column == at * heads + a, stat, stats)
        out[to, :, cols:] = stats.reshape(some // high, high, DH)


def query_part(scal, asked, near, far, shards, n, after):
    rows, cols = asked.shape
    width = near.shape[0]
    kv_heads = near.shape[1] // (2 * DH)
    key = pl.BlockSpec((width, DH), lambda i, s: (0, s[0]))
    value = pl.BlockSpec((width, DH), lambda i, s: (0, kv_heads + s[0]))
    result = (n, rows // n, cols + DH)
    return pl.pallas_call(
        functools.partial(query_kernel, shards),
        out_shape=jax.ShapeDtypeStruct(result, jnp.float32),
        grid_spec=pltpu.PrefetchScalarGridSpec(
            num_scalar_prefetch=1,
            grid=(1,),
            in_specs=[pl.BlockSpec((rows, cols), lambda i, s: (0, 0)), key, key, value, value]
            + [pl.BlockSpec(memory_space=pl.ANY)],
            out_specs=pl.BlockSpec(result, lambda i, s: (0, 0, 0)),
            scratch_shapes=[pltpu.VMEM((2 * width, 2 * DH), jnp.bfloat16)],
        ),
        compiler_params=pltpu.CompilerParams(vmem_limit_bytes=40 * 2**20),
        cost_estimate=pl.CostEstimate(flops=2**31, bytes_accessed=2**22, transcendentals=2**21),
        name="query_part",
    )(scal, asked, near, far, near, far, after)


def merge_kernel(parts, out):
    heads = out.shape[2] // DH

    def stat(at, a):
        lane = heads * DH + at * heads + a
        return parts[:, :, lane : lane + 1]

    for a in range(heads):
        top = stat(0, a) + stat(1, a) + stat(2, a)
        total = stat(3, a) + stat(4, a) + stat(5, a)
        best = jnp.max(top, axis=0, keepdims=True)
        scale = jnp.exp2(top - best)
        total_all = jnp.sum(total * scale, axis=0)
        scale = scale * jnp.exp2(stat(6, a))
        summed = jnp.sum(parts[:, :, a * DH : (a + 1) * DH] * scale, axis=0)
        done = (summed / total_all).astype(out.dtype)
        out[:, :, a * DH : (a + 1) * DH] = jnp.broadcast_to(done[None], (out.shape[0],) + done.shape)


def merge_parts(parts):
    n, rows, cols = parts.shape
    return pl.pallas_call(
        merge_kernel,
        out_shape=jax.ShapeDtypeStruct((n, rows, cols - DH), jnp.bfloat16),
        compiler_params=pltpu.CompilerParams(vmem_limit_bytes=40 * 2**20),
        cost_estimate=pl.CostEstimate(flops=2**20, bytes_accessed=2**21, transcendentals=2**10),
        name="merge_parts",
    )(parts)


def context_kernel(shards, scal, query, *refs):
    keys, values, out, value = refs[:4], refs[4:8], refs[8], refs[9]
    own, length, hst = scal[0], scal[1], scal[2]
    rows, heads = query.shape[0], query.shape[1] // DH
    key = jnp.concatenate([r[...] for r in keys], axis=0)
    value[:, :DH] = jnp.concatenate([r[...] for r in values], axis=0)
    many = key.shape[0]

    @pl.when(pl.program_id(0) == 0)
    def _():
        value[:, DH:] = jnp.ones((many, DH), jnp.bfloat16)

    row = lax.broadcasted_iota(jnp.int32, (rows, rows), 0)
    diagonal = lax.broadcasted_iota(jnp.int32, (rows, rows), 1) <= row
    dropped = [jnp.where(scal[3 + j] < own, 0.0, NEG) for j in range(1, shards)]
    bias = [jnp.full((1, rows), d, jnp.float32) for d in dropped]
    front = many - shards * rows
    bias = jnp.concatenate(bias + [jnp.full((1, front), jnp.where(hst > 0, 0.0, NEG), jnp.float32)], axis=1)
    live = own * rows + row < length
    for a in range(heads):
        column = slice(a * DH, (a + 1) * DH)
        score = lax.dot_general(
            query[:, column], key, (((1,), (1,)), ((), ())), preferred_element_type=jnp.float32
        )
        score = jnp.concatenate(
            [jnp.where(diagonal, score[:, :rows], NEG), score[:, rows:] + bias], axis=1
        )
        top = jnp.max(score, axis=1, keepdims=True)
        weight = jnp.exp2((score - top) * EXP2_SCALE).astype(jnp.bfloat16)
        summed = jnp.dot(weight, value[...], preferred_element_type=jnp.float32)
        out[:, column] = jnp.where(live, summed[:, :DH] / summed[:, DH:], 0.0).astype(out.dtype)


def context_part(scal, query, parts, shards, first, count, before, after, flops):
    rows, cols = query.shape
    kv_heads = parts[0].shape[1] // (2 * DH)
    group = cols // kv_heads

    def specs(offset):
        return [pl.BlockSpec((p.shape[0], DH), lambda g, s: (0, first + g + offset)) for p in parts]

    wide = pl.BlockSpec((rows, group), lambda g, s: (0, first + g))
    extra = ([] if before is None else [before]) + after

    def kernel(scal, query, *refs):
        context_kernel(shards, scal, query, *refs[: 2 * len(parts)], *refs[2 * len(parts) + len(extra) :])

    return pl.pallas_call(
        kernel,
        out_shape=jax.ShapeDtypeStruct((rows, cols), jnp.bfloat16),
        grid_spec=pltpu.PrefetchScalarGridSpec(
            num_scalar_prefetch=1,
            grid=(count,),
            in_specs=[wide] + specs(0) + specs(kv_heads) + [pl.BlockSpec(memory_space=pl.ANY)] * len(extra),
            out_specs=wide,
            scratch_shapes=[pltpu.VMEM((sum(p.shape[0] for p in parts), 2 * DH), jnp.bfloat16)],
        ),
        input_output_aliases={} if before is None else {2 + 2 * len(parts): 0},
        compiler_params=pltpu.CompilerParams(vmem_limit_bytes=62 * 2**20),
        cost_estimate=pl.CostEstimate(flops=flops, bytes_accessed=2**10, transcendentals=0),
        name="context_part",
    )(scal, query, *parts, *parts, *extra)


def per_device(n_hst, n_head, ny, ctx_query, ctx_key, ctx_value, requests, lengths, owner):
    hst, head = lax.axis_index("hst"), lax.axis_index("head")
    chips = n_head // CORES
    pieces = requests[0].reshape(n_hst, -1, requests.shape[2])
    scattered = lax.all_to_all(pieces, "hst", 0, 0)
    piece = lax.dynamic_index_in_dim(scattered, owner[0], 0, False)
    asked = lax.all_to_all(jnp.broadcast_to(piece[None], pieces.shape), "hst", 0, 0)
    asked = asked.reshape(requests.shape[1:])
    kv = jnp.concatenate([ctx_key, ctx_value], axis=1)
    near, far = spread_over_group(kv, chips)
    anchor = spread_anchor(kv, hst, head, n_hst, n_head, ny)
    near_anchor, far_anchor = spread_over_group(anchor, chips)
    x, core = head // CORES, head % CORES
    places = [((x - step) % chips) * CORES + c for c in (core, 1 - core) for step in range(chips)]
    scal = jnp.stack([head, lengths[0], hst] + places).astype(jnp.int32)
    part = query_part(scal, asked, near, far, n_head, n_hst, anchor).astype(jnp.float16)
    parts = lax.all_to_all(part, "hst", 0, 0).astype(jnp.float32)
    kv_parts = [near, far, near_anchor, far_anchor]
    begun = context_part(scal, ctx_query, kv_parts, n_head, 0, 2, None, [], 2**20)
    parts, begun = lax.optimization_barrier((parts, begun))
    done = merge_parts(parts)
    query_out = lax.all_to_all(done, "hst", 0, 0)
    context_out = context_part(scal, ctx_query, kv_parts, n_head, 2, n_head - 2, begun, [], 2**34)
    return context_out, query_out.reshape(requests.shape[1:])


def solution(mesh):
    placed = (
        P(("hst", "head"), None),
        P(("hst", "head"), None),
        P(("hst", "head"), None),
        P("hst", None, "head"),
        P("hst"),
        P(),
    )
    return jax.shard_map(
        functools.partial(per_device, mesh.shape["hst"], mesh.shape["head"], 4),
        mesh=mesh,
        in_specs=placed,
        out_specs=(P(("hst", "head"), None), P(None, "head")),
        check_vma=False,
    )
```

```python
import functools

import jax
import jax.numpy as jnp
from jax import lax
from jax.experimental import pallas as pl
from jax.experimental.pallas import tpu as pltpu
from jax.sharding import PartitionSpec as P

DH = 128
CORES = 2
NEG = -1e30
EXP2_SCALE = DH ** (-0.5) * 1.4426950408889634


def spread_over_group(shard, chips):
    size = chips * CORES
    ring = [
        lax.ppermute(shard, "head", [(i, (i + step * CORES) % size) for i in range(size)])
        for step in range(1, chips)
    ]
    near = jnp.concatenate([shard] + ring, axis=0)
    return near, lax.ppermute(near, "head", [(i, i ^ 1) for i in range(size)])


def spread_anchor(kv, hst, head, n_hst, n_head, ny):
    rows = kv.shape[0] // 2
    sources = n_head // 2
    moved = lax.ppermute(kv[rows:], ("hst", "head"), [(h, h + sources) for h in range(sources)])
    part = jnp.where(head < sources, kv[:rows], moved)
    z, y = hst // ny, hst % ny

    def send(x, pairs):
        return lax.ppermute(x, "hst", [(a * ny, b * ny) for a, b in pairs])

    first, second = send(part, [(0, 3)]), send(part, [(0, 5)])
    part = jnp.where(z == 3, first, jnp.where(z == 5, second, part))
    first, second = send(part, [(0, 1), (3, 4), (5, 6)]), send(part, [(0, 7), (3, 2)])
    part = jnp.where((z == 1) | (z == 4) | (z == 6), first, jnp.where((z == 7) | (z == 2), second, part))
    groups = range(n_hst // ny)
    first, second, third = (
        lax.ppermute(part, "hst", [(k * ny, k * ny + to) for k in groups]) for to in (1, 3, 2)
    )
    return jnp.where(y == 1, first, jnp.where(y == 3, second, jnp.where(y == 2, third, part)))


def pieces_of(x):
    parts = []
    for _ in range(3):
        parts.append(x.astype(jnp.bfloat16).astype(jnp.float32))
        x = x - parts[-1]
    return parts


def query_kernel(shards, scal, asked, near_key, far_key, near_value, far_value, after, out, value):
    length = scal[1]
    rows, cols = asked.shape
    heads = cols // DH
    key = jnp.concatenate([near_key[...], far_key[...]], axis=0)
    many = key.shape[0]
    value[:, :DH] = jnp.concatenate([near_value[...], far_value[...]], axis=0)
    value[:, DH:] = jnp.ones((many, DH), jnp.bfloat16)
    width = many // shards
    lane = lax.broadcasted_iota(jnp.int32, (1, width), 1)
    keep = jnp.concatenate([lane + scal[3 + j] * width for j in range(shards)], axis=1) < length
    some = 128
    column = lax.broadcasted_iota(jnp.int32, (some, DH), 1)
    high = out.shape[1]
    for first in range(0, rows, some):
        to = slice(first // high, (first + some) // high)
        stats = jnp.zeros((some, DH), jnp.float32)
        for a in range(heads):
            mine = slice(a * DH, (a + 1) * DH)
            score = lax.dot_general(
                asked[first : first + some, mine],
                key,
                (((1,), (1,)), ((), ())),
                preferred_element_type=jnp.float32,
            )
            score = jnp.where(keep, score, NEG)
            top = jnp.max(score, axis=1, keepdims=True)
            weight = jnp.exp2((score - top) * EXP2_SCALE).astype(jnp.bfloat16)
            both = jnp.dot(weight, value[...], preferred_element_type=jnp.float32)
            summed, total = both[:, :DH], both[:, DH:]
            reach = jnp.max(jnp.abs(summed), axis=1, keepdims=True)
            power = jnp.ceil(jnp.log2(jnp.maximum(reach, 1e-36)))
            out[to, :, mine] = (summed * jnp.exp2(-power)).reshape(some // high, high, DH)
            values = pieces_of(top * EXP2_SCALE) + pieces_of(total) + [power]
            for at, stat in enumerate(values):
                stats = jnp.where(column == at * heads + a, stat, stats)
        out[to, :, cols:] = stats.reshape(some // high, high, DH)


def query_part(scal, asked, near, far, shards, n, after):
    rows, cols = asked.shape
    width = near.shape[0]
    kv_heads = near.shape[1] // (2 * DH)
    key = pl.BlockSpec((width, DH), lambda i, s: (0, s[0]))
    value = pl.BlockSpec((width, DH), lambda i, s: (0, kv_heads + s[0]))
    result = (n, rows // n, cols + DH)
    return pl.pallas_call(
        functools.partial(query_kernel, shards),
        out_shape=jax.ShapeDtypeStruct(result, jnp.float32),
        grid_spec=pltpu.PrefetchScalarGridSpec(
            num_scalar_prefetch=1,
            grid=(1,),
            in_specs=[pl.BlockSpec((rows, cols), lambda i, s: (0, 0)), key, key, value, value]
            + [pl.BlockSpec(memory_space=pl.ANY)],
            out_specs=pl.BlockSpec(result, lambda i, s: (0, 0, 0)),
            scratch_shapes=[pltpu.VMEM((2 * width, 2 * DH), jnp.bfloat16)],
        ),
        compiler_params=pltpu.CompilerParams(vmem_limit_bytes=40 * 2**20),
        cost_estimate=pl.CostEstimate(flops=2**31, bytes_accessed=2**22, transcendentals=2**21),
        name="query_part",
    )(scal, asked, near, far, near, far, after)


def merge_kernel(parts, out):
    heads = out.shape[2] // DH
    stats = parts[:, :, heads * DH :]

    def lane(x, at):
        return pltpu.roll(x, (DH - at * heads) % DH, 2)

    whole = stats + lane(stats, 1) + lane(stats, 2)
    top, total = whole, lane(whole, 3)
    front = lax.broadcasted_iota(jnp.int32, stats.shape, 2) < heads
    scale = jnp.where(front, jnp.exp2(top - jnp.max(top, axis=0, keepdims=True)), 0.0)
    total_all = jnp.sum(total * scale, axis=0, keepdims=True)
    power = jnp.where(front, lane(stats, 6), 0.0)
    factor = scale * jnp.exp2(power) / jnp.where(front[:1], total_all, 1.0)
    for a in range(heads):
        column = slice(a * DH, (a + 1) * DH)
        done = jnp.sum(parts[:, :, column] * factor[:, :, a : a + 1], axis=0).astype(out.dtype)
        out[:, :, column] = jnp.broadcast_to(done[None], (out.shape[0],) + done.shape)


def merge_parts(parts):
    n, rows, cols = parts.shape
    return pl.pallas_call(
        merge_kernel,
        out_shape=jax.ShapeDtypeStruct((n, rows, cols - DH), jnp.bfloat16),
        compiler_params=pltpu.CompilerParams(vmem_limit_bytes=40 * 2**20),
        cost_estimate=pl.CostEstimate(flops=2**20, bytes_accessed=2**21, transcendentals=2**10),
        name="merge_parts",
    )(parts)


def context_kernel(shards, scal, query, *refs):
    keys, values, out, value = refs[:4], refs[4:8], refs[8], refs[9]
    own, length, hst = scal[0], scal[1], scal[2]
    rows, heads = query.shape[0], query.shape[1] // DH
    key = jnp.concatenate([r[...] for r in keys], axis=0)
    value[:, :DH] = jnp.concatenate([r[...] for r in values], axis=0)
    many = key.shape[0]

    @pl.when(pl.program_id(0) == 0)
    def _():
        value[:, DH:] = jnp.ones((many, DH), jnp.bfloat16)

    row = lax.broadcasted_iota(jnp.int32, (rows, rows), 0)
    diagonal = lax.broadcasted_iota(jnp.int32, (rows, rows), 1) <= row
    dropped = [jnp.where(scal[3 + j] < own, 0.0, NEG) for j in range(1, shards)]
    bias = [jnp.full((1, rows), d, jnp.float32) for d in dropped]
    front = many - shards * rows
    bias = jnp.concatenate(bias + [jnp.full((1, front), jnp.where(hst > 0, 0.0, NEG), jnp.float32)], axis=1)
    live = own * rows + row < length
    for a in range(heads):
        column = slice(a * DH, (a + 1) * DH)
        score = lax.dot_general(
            query[:, column], key, (((1,), (1,)), ((), ())), preferred_element_type=jnp.float32
        )
        score = jnp.concatenate(
            [jnp.where(diagonal, score[:, :rows], NEG), score[:, rows:] + bias], axis=1
        )
        top = jnp.max(score, axis=1, keepdims=True)
        weight = jnp.exp2((score - top) * EXP2_SCALE).astype(jnp.bfloat16)
        summed = jnp.dot(weight, value[...], preferred_element_type=jnp.float32)
        out[:, column] = jnp.where(live, summed[:, :DH] / summed[:, DH:], 0.0).astype(out.dtype)


def context_part(scal, query, parts, shards, first, count, before, after, flops):
    rows, cols = query.shape
    kv_heads = parts[0].shape[1] // (2 * DH)
    group = cols // kv_heads

    def specs(offset):
        return [pl.BlockSpec((p.shape[0], DH), lambda g, s: (0, first + g + offset)) for p in parts]

    wide = pl.BlockSpec((rows, group), lambda g, s: (0, first + g))
    extra = ([] if before is None else [before]) + after

    def kernel(scal, query, *refs):
        context_kernel(shards, scal, query, *refs[: 2 * len(parts)], *refs[2 * len(parts) + len(extra) :])

    return pl.pallas_call(
        kernel,
        out_shape=jax.ShapeDtypeStruct((rows, cols), jnp.bfloat16),
        grid_spec=pltpu.PrefetchScalarGridSpec(
            num_scalar_prefetch=1,
            grid=(count,),
            in_specs=[wide] + specs(0) + specs(kv_heads) + [pl.BlockSpec(memory_space=pl.ANY)] * len(extra),
            out_specs=wide,
            scratch_shapes=[pltpu.VMEM((sum(p.shape[0] for p in parts), 2 * DH), jnp.bfloat16)],
        ),
        input_output_aliases={} if before is None else {2 + 2 * len(parts): 0},
        compiler_params=pltpu.CompilerParams(vmem_limit_bytes=62 * 2**20),
        cost_estimate=pl.CostEstimate(flops=flops, bytes_accessed=2**10, transcendentals=0),
        name="context_part",
    )(scal, query, *parts, *parts, *extra)


def per_device(n_hst, n_head, ny, ctx_query, ctx_key, ctx_value, requests, lengths, owner):
    hst, head = lax.axis_index("hst"), lax.axis_index("head")
    chips = n_head // CORES
    pieces = requests[0].reshape(n_hst, -1, requests.shape[2])
    scattered = lax.all_to_all(pieces, "hst", 0, 0)
    piece = lax.dynamic_index_in_dim(scattered, owner[0], 0, False)
    asked = lax.all_to_all(jnp.broadcast_to(piece[None], pieces.shape), "hst", 0, 0)
    asked = asked.reshape(requests.shape[1:])
    kv = jnp.concatenate([ctx_key, ctx_value], axis=1)
    near, far = spread_over_group(kv, chips)
    anchor = spread_anchor(kv, hst, head, n_hst, n_head, ny)
    near_anchor, far_anchor = spread_over_group(anchor, chips)
    x, core = head // CORES, head % CORES
    places = [((x - step) % chips) * CORES + c for c in (core, 1 - core) for step in range(chips)]
    scal = jnp.stack([head, lengths[0], hst] + places).astype(jnp.int32)
    part = query_part(scal, asked, near, far, n_head, n_hst, anchor).astype(jnp.float16)
    parts = lax.all_to_all(part, "hst", 0, 0).astype(jnp.float32)
    kv_parts = [near, far, near_anchor, far_anchor]
    begun = context_part(scal, ctx_query, kv_parts, n_head, 0, 2, None, [], 2**20)
    parts, begun = lax.optimization_barrier((parts, begun))
    done = merge_parts(parts)
    query_out = lax.all_to_all(done, "hst", 0, 0)
    context_out = context_part(scal, ctx_query, kv_parts, n_head, 2, n_head - 2, begun, [], 2**34)
    return context_out, query_out.reshape(requests.shape[1:])


def solution(mesh):
    placed = (
        P(("hst", "head"), None),
        P(("hst", "head"), None),
        P(("hst", "head"), None),
        P("hst", None, "head"),
        P("hst"),
        P(),
    )
    return jax.shard_map(
        functools.partial(per_device, mesh.shape["hst"], mesh.shape["head"], 4),
        mesh=mesh,
        in_specs=placed,
        out_specs=(P(("hst", "head"), None), P(None, "head")),
        check_vma=False,
    )
```
